32 devices in a mesh: row: 8 (over z, x), col: 4 (over y, core).
Axes of the slice: x: 2, y: 2, z: 4, core: 2. Of those that a mesh axis runs over, the one named last changes fastest.
Arguments:
- t_upper: bfloat16 [3, 4096, 4096], P(None, 'row', 'col'), may hold values from -0.03125 to 0.03125
- t_old: bfloat16 [3, 4096, 24576], P(None, 'row', 'col'), may hold values from -0.03125 to 0.03125
- inverses: bfloat16 [3, 4096, 4096], P(None, 'row', 'col'), may hold values from -1 to 1.5, as said below
- forcing: float32 [3, 4096, 128], P(None, 'row'), may hold values from -6 to 6
- x_old: bfloat16 [24576, 128], P('col'), may hold values from -6 to 6
- offsets: float32 [128], replicated, may hold values from -0.5 to 0.5
- starts: int32 [128], replicated, may hold values from 0 to 36864
- column_map: int32 [128], replicated, may hold values from 0 to 127, each once
- z_cols: bfloat16 [49152, 3, 4096], P('row', None, 'col'), may hold values from -0.0546875 to 0.0546875
- acc: float32 [49152, 128], P(('row', 'col')), may hold values from -6 to 6
Outputs:
- solved: float32 [3, 4096, 128], P(None, ('row', 'col'))
- acc_out: float32 [49152, 128], P(('row', 'col'))
The draws below stay inside these ranges and needn't reach their ends.
Inputs may be any that keep to these rules, and one draw needn't show every extreme that they name: `inverses`: dense matrices with a dominant positive diagonal.
All inputs are finite; a program needn't handle non-finite values.
Results may differ from the reference program's by a relative error of at most 0.0003.
Values may be sent and summed in bfloat16 or wider, within the bound.
A program may use at most 192 MiB of HBM per device.

```python
import jax
import jax.numpy as jnp
from jax import lax

B = 4096
STEPS = 3
NEUMANN = 3
E = 128
K = 24576
NZ = 49152


def draw_inverses(key, part):
    key_diag = jax.random.fold_in(key, 11)
    key_off = jax.random.fold_in(key, 12)
    diag = jnp.exp(jax.random.uniform(key_diag, (STEPS, B), jnp.float32, jnp.log(0.5), 0.0))
    spread = jax.random.normal(key_off, (STEPS, B, B), jnp.float32) * (0.3 / B ** 0.5)
    eye = jnp.eye(B, dtype=jnp.float32)
    whole = spread + diag[:, :, None] * eye[None, :, :]
    return jnp.clip(whole, -1.0, 1.5).astype(jnp.bfloat16)


def touch_ends(entries, stream_key, low, largest):
    index_at = [jax.random.randint(jax.random.fold_in(stream_key, axis), (), 0, length) for axis, length in enumerate(entries.shape)]
    widest = entries.shape.index(max(entries.shape))
    next_to = index_at[:widest] + [(index_at[widest] + 1) % entries.shape[widest]] + index_at[widest + 1:]
    return entries.at[tuple(index_at)].set(low).at[tuple(next_to)].set(largest)


def level_of(rng, extent, split, low, largest):
    loudness, own = 1.0, jax.random.fold_in(rng, 6)
    for dim, blocks in split:
        steps = jnp.exp(jax.random.uniform(jax.random.fold_in(own, dim), (blocks,), jnp.float32, low / len(split), largest / len(split)))
        loudness = loudness * jnp.repeat(steps, extent[dim] // blocks).reshape([-1 if axis == dim else 1 for axis in range(len(extent))])
    return loudness


def normal_values(stream_key, shape, scale, most, cuts=(), kind=jnp.bfloat16):
    result = scale * jax.random.normal(stream_key, shape, jnp.float32)
    if cuts:
        result = result * level_of(stream_key, shape, cuts, -0.22, 0.18)
    return jnp.clip(result, -most, most).astype(kind)


def setup_inputs(seed: int = 0) -> dict:
    keys = jax.random.split(jax.random.key(seed), 11)
    return {
        "t_upper": normal_values(keys[0], (3, B, B), (2 * B + K) ** -0.5, 0.03125, ((1, 8), (2, 4))),
        "t_old": normal_values(keys[1], (STEPS, B, K), (2 * B + K) ** -0.5, 0.03125, ((1, 8), (2, 4))),
        "inverses": draw_inverses(jax.random.fold_in(keys[10], 71), 0),
        "forcing": normal_values(keys[3], (STEPS, B, E), 1.0, 6.0, ((1, 8),), jnp.float32),
        "x_old": normal_values(keys[4], (K, E), 1.0, 6.0, ((0, 4),)),
        "offsets": jnp.clip(jax.random.uniform(keys[5], (E,), jnp.float32, -0.5, 0.5), -0.5, 0.5),
        "starts": touch_ends(jax.random.randint(keys[6], (E,), 0, STEPS * B + K + 1), jax.random.fold_in(keys[6], 1), 0, STEPS * B + K).astype(jnp.int32),
        "column_map": jax.random.permutation(keys[7], E).astype(jnp.int32),
        "z_cols": normal_values(keys[8], (NZ, STEPS, B), (STEPS * B) ** -0.5, 0.0546875, ((0, 8), (2, 4))),
        "acc": normal_values(keys[9], (NZ, E), 1.0, 6.0, ((0, 32),), jnp.float32),
    }


def split_pair(values):
    upper = values.astype(jnp.bfloat16)
    lower = (values - lax.optimization_barrier(upper).astype(jnp.float32)).astype(jnp.bfloat16)
    return jnp.concatenate([upper, lower], axis=-1)


def fold_pair(product):
    return product[:, :E] + product[:, E:]


def reference(t_upper, t_old, inverses, forcing, x_old, offsets, starts, column_map, z_cols, acc):
    pairs = {}
    count = 0
    for first in range(STEPS):
        for second in range(first + 1, STEPS):
            pairs[(first, second)] = count
            count = count + 1
    old_rows = STEPS * B + jnp.arange(K, dtype=jnp.int32)
    old_live = old_rows[:, None] < starts[None, :]
    old_vals = jnp.where(old_live, x_old, jnp.zeros_like(x_old))
    results = [None] * STEPS
    rounded = [None] * STEPS
    for step in reversed(range(STEPS)):
        rhs = forcing[step] - jnp.dot(t_old[step], old_vals, preferred_element_type=jnp.float32)
        for later in range(step + 1, STEPS):
            rhs = rhs - fold_pair(jnp.dot(t_upper[pairs[(step, later)]], rounded[later], preferred_element_type=jnp.float32))
        term = fold_pair(jnp.dot(inverses[step], split_pair(rhs), preferred_element_type=jnp.float32))
        total = term
        for extra in range(1, NEUMANN):
            term = fold_pair(jnp.dot(inverses[step], split_pair(term), preferred_element_type=jnp.float32)) * offsets[None, :]
            total = total + term
        rows = step * B + jnp.arange(B, dtype=jnp.int32)
        total = jnp.where(rows[:, None] < starts[None, :], total, jnp.zeros_like(total))
        results[step] = total
        rounded[step] = split_pair(total)
    stacked = jnp.stack(rounded)
    index = jnp.concatenate([column_map, column_map + E]).astype(jnp.int32)
    picked = stacked[:, :, index].reshape(STEPS * B, 2 * E)
    contribution = fold_pair(jnp.dot(z_cols.reshape(NZ, STEPS * B), picked, preferred_element_type=jnp.float32))
    return jnp.stack(results), acc + contribution
```

```python
import functools

import jax
import jax.numpy as jnp
from jax import lax
from jax.experimental import pallas as pl
from jax.experimental.pallas import tpu as pltpu
from jax.sharding import PartitionSpec as P

NEUMANN = 3
MESH = pl.DeviceIdType.MESH


def pair_indices(steps):
    pairs = {}
    for first in range(steps):
        for second in range(first + 1, steps):
            pairs[first, second] = len(pairs)
    return pairs


def chain_kernel(
    n_row, n_col, upper_ref, inv_ref, old_ref, forcing_ref, offsets_ref, starts_ref,
    solved_ref, xs_ref,
    part_out, part_in, pair_out, pair_in,
    part_send, part_recv, pair_send, pair_recv,
):
    row = lax.axis_index("row")
    col = lax.axis_index("col")
    steps, row_block, width = old_ref.shape
    col_block = upper_ref.shape[2]
    share = row_block // n_col
    ratio = col_block // row_block
    pairs = pair_indices(steps)
    owner_col = row // ratio
    has_self = owner_col == col
    place = lax.rem(row, ratio) * row_block + col * share
    place = pl.multiple_of(place, share)

    barrier = pltpu.get_barrier_semaphore()
    for hop in range(1, n_col):
        pl.semaphore_signal(
            barrier, inc=1, device_id={"row": row, "col": lax.rem(col + hop, n_col)}, device_id_type=MESH
        )
    for extra in range(ratio):
        for source in range(n_col):
            source_row = col * ratio + extra

            @pl.when(jnp.logical_or(source_row != row, source != col))
            def _():
                pl.semaphore_signal(
                    barrier, inc=1, device_id={"row": source_row, "col": source}, device_id_type=MESH
                )

    pl.semaphore_wait(barrier, n_col - 1 + n_row - jnp.where(has_self, 1, 0))

    def fold(product):
        return product[:, :width] + product[:, width:]

    def reduce_rows(k, block):
        copies = []
        for hop in range(n_col - 1, 0, -1):
            target = lax.rem(col + hop, n_col)
            part_out[k, hop - 1] = block(target)
            copy = pltpu.make_async_remote_copy(
                src_ref=part_out.at[k, hop - 1],
                dst_ref=part_in.at[k, hop - 1],
                send_sem=part_send.at[k, hop - 1],
                recv_sem=part_recv.at[k, hop - 1],
                device_id={"row": row, "col": target},
                device_id_type=MESH,
            )
            copy.start()
            copies.append((hop, copy))
        value = block(col)
        for hop, copy in copies:
            copy.wait()
            value = value + part_in[k, hop - 1]
        return value

    def start_spread(k, value):
        upper = value.astype(jnp.bfloat16)
        lower = (value - upper.astype(jnp.float32)).astype(jnp.bfloat16)
        pair_out[k, :, :width] = upper
        pair_out[k, :, width:] = lower
        for hop in range(n_row):
            target = lax.rem(row + hop + 1, n_row)

            def send():
                pltpu.make_async_remote_copy(
                    src_ref=pair_out.at[k],
                    dst_ref=pair_in.at[k, pl.ds(place, share)],
                    send_sem=pair_send.at[k],
                    recv_sem=pair_recv.at[k],
                    device_id={"row": target, "col": owner_col},
                    device_id_type=MESH,
                ).start()

            if hop < n_row - 1:
                send()
            else:
                pl.when(jnp.logical_not(has_self))(send)

        @pl.when(has_self)
        def _():
            pair_in[k, pl.ds(place, share), :width] = upper
            pair_in[k, pl.ds(place, share), width:] = lower

    def wait_all(k, sem):
        for mine, rows in ((True, col_block - share), (False, col_block)):

            @pl.when(has_self == mine)
            def _():
                span = pair_in.at[k, pl.ds(0, rows)]
                pltpu.make_async_copy(span, span, sem.at[k]).wait()

    def spread(k, value):
        start_spread(k, value)
        wait_all(k, pair_recv)

    def times(mat_ref, index, k):
        def block(target):
            rows = pl.ds(pl.multiple_of(target * share, share), share)
            return fold(
                jnp.dot(mat_ref[index, rows, :], pair_in[k], preferred_element_type=jnp.float32)
            )

        return block

    offsets = offsets_ref[...]
    starts = starts_ref[...]
    k = 0
    solved_at = {}
    for step in reversed(range(steps)):

        def rhs_block(target):
            rows = pl.ds(pl.multiple_of(target * share, share), share)
            value = -old_ref[step, rows, :]
            for later in range(step + 1, steps):
                value = value - times(upper_ref, pairs[step, later], solved_at[later])(target)
            return value

        mine = pl.ds(pl.multiple_of(col * share, share), share)
        rhs = reduce_rows(k, rhs_block) + forcing_ref[step, mine, :]
        spread(k, rhs)
        k += 1
        total = None
        for term_index in range(NEUMANN):
            term = reduce_rows(k, times(inv_ref, step, k - 1))
            if term_index:
                term = term * offsets
            total = term if total is None else total + term
            if term_index < NEUMANN - 1:
                spread(k, term)
                k += 1
        first = step * (col_block * n_col) + row * row_block + col * share
        rows = first + lax.broadcasted_iota(jnp.int32, (share, width), 0)
        total = jnp.where(rows < starts, total, 0.0)
        solved_ref[step] = total
        spread(k, total)
        solved_at[step] = k
        k += 1
        xs_ref[step] = pair_in[solved_at[step]]
    for slot in range(k):
        wait_all(slot, pair_send)


def chain(n_row, n_col, t_upper, inverses, old_part, forcing, offsets, starts):
    steps, row_block, width = old_part.shape
    col_block = t_upper.shape[2]
    share = row_block // n_col
    rounds = steps * (NEUMANN + 1)
    vmem = pl.BlockSpec(memory_space=pltpu.VMEM)
    return pl.pallas_call(
        functools.partial(chain_kernel, n_row, n_col),
        out_shape=(
            jax.ShapeDtypeStruct((steps, share, width), jnp.float32),
            jax.ShapeDtypeStruct((steps, col_block, 2 * width), jnp.bfloat16),
        ),
        in_specs=[vmem] * 6,
        out_specs=(vmem, vmem),
        scratch_shapes=[
            pltpu.VMEM((rounds, n_col - 1, share, width), jnp.float32),
            pltpu.VMEM((rounds, n_col - 1, share, width), jnp.float32),
            pltpu.VMEM((rounds, share, 2 * width), jnp.bfloat16),
            pltpu.VMEM((rounds, col_block, 2 * width), jnp.bfloat16),
            pltpu.SemaphoreType.DMA((rounds, n_col - 1)),
            pltpu.SemaphoreType.DMA((rounds, n_col - 1)),
            pltpu.SemaphoreType.DMA((rounds,)),
            pltpu.SemaphoreType.DMA((rounds,)),
        ],
        compiler_params=pltpu.CompilerParams(
            collective_id=0, has_side_effects=True, vmem_limit_bytes=48 * 1024 * 1024
        ),
        name="chain",
    )(t_upper, inverses, old_part, forcing, offsets, starts)


def body(t_upper, t_old, inverses, forcing, x_old, offsets, starts, column_map, z_cols, acc):
    n_col = lax.axis_size("col")
    n_row = lax.axis_size("row")
    col_idx = lax.axis_index("col")
    steps, row_block, width = forcing.shape
    col_block = t_upper.shape[2]
    old_cols = x_old.shape[0]
    full_rows = col_block * n_col

    old_rows = steps * full_rows + col_idx * old_cols + jnp.arange(old_cols, dtype=jnp.int32)
    old_live = old_rows[:, None] < starts[None, :]
    old_vals = jnp.where(old_live, x_old, jnp.zeros_like(x_old))
    old_part = jnp.dot(
        t_old.reshape(steps * row_block, old_cols), old_vals, preferred_element_type=jnp.float32
    ).reshape(steps, row_block, width)
    solved, stacked = chain(
        n_row, n_col, t_upper, inverses, old_part, forcing, offsets[None, :], starts[None, :]
    )
    one_hot = (jnp.arange(width, dtype=jnp.int32)[:, None] == column_map[None, :]).astype(
        jnp.bfloat16
    )
    picked = jnp.concatenate(
        [
            jnp.dot(stacked[..., :width], one_hot, preferred_element_type=jnp.float32),
            jnp.dot(stacked[..., width:], one_hot, preferred_element_type=jnp.float32),
        ],
        axis=-1,
    ).astype(jnp.bfloat16)
    by_step = jnp.transpose(z_cols, (1, 0, 2))
    product = sum(
        jnp.dot(by_step[step], picked[step], preferred_element_type=jnp.float32)
        for step in range(steps)
    )
    contribution = lax.psum_scatter(
        product[:, :width] + product[:, width:], "col", scatter_dimension=0, tiled=True
    )
    return (solved, acc + contribution)


def solution(mesh):
    placed = (
        P(None, "row", "col"),
        P(None, "row", "col"),
        P(None, "row", "col"),
        P(None, "row", None),
        P("col", None),
        P(),
        P(),
        P(),
        P("row", None, "col"),
        P(("row", "col"), None),
    )
    return jax.shard_map(
        body,
        mesh=mesh,
        in_specs=placed,
        out_specs=(P(None, ("row", "col"), None), P(("row", "col"), None)),
        check_vma=False,
    )
```

```python
import functools
import math

import jax
import jax.numpy as jnp
from jax import lax
from jax.experimental import pallas as pl
from jax.experimental.pallas import tpu as pltpu
from jax.sharding import PartitionSpec as P

NEUMANN = 3
PIECES = 4
OLD_PARTS = 2
MESH = pl.DeviceIdType.MESH


def pair_indices(steps):
    pairs = {}
    for first in range(steps):
        for second in range(first + 1, steps):
            pairs[first, second] = len(pairs)
    return pairs


def chain_kernel(
    n_row, n_col,
    upper_hbm, inv_hbm, old_hbm, z_hbm,
    forcing_ref, x_old_ref, offsets_ref, starts_ref, map_ref, acc_ref,
    solved_ref, acc_out_ref,
    upper_ref, inv_ref, old_buf, z_buf, x_live, old_sum, sel, z_sum,
    part_out, part_in, pair_out, pair_in, core_in, chip_in,
    load_sem, old_sem, z_sem,
    part_send, part_recv, pair_send, pair_recv, pass_send, pass_recv,
    core_send, core_recv, chip_send, chip_recv,
):
    row = lax.axis_index("row")
    col = lax.axis_index("col")
    steps, row_block, width = forcing_ref.shape
    col_block = upper_ref.shape[2]
    share = row_block // n_col
    ratio = col_block // row_block
    old_cols = x_old_ref.shape[0]
    chunk = z_sum.shape[1]
    pairs = pair_indices(steps)
    base_row = row // ratio
    sub_row = lax.rem(row, ratio)
    owner_col = base_row
    has_self = owner_col == col
    groups = n_row // ratio
    place = pl.multiple_of(sub_row * row_block + col * share, share)

    old_cut = old_cols // OLD_PARTS

    def old_copy(index):
        step = steps - 1 - index // OLD_PARTS
        half = index % OLD_PARTS
        slot = index % 2
        return pltpu.make_async_copy(
            old_hbm.at[step, :, pl.ds(half * old_cut, old_cut)], old_buf.at[slot], old_sem.at[slot]
        )

    def z_copy(step, index):
        first = index * chunk
        if not isinstance(index, int):
            first = pl.multiple_of(first, chunk)
        return pltpu.make_async_copy(
            z_hbm.at[step, pl.ds(first, chunk)], z_buf.at[index], z_sem.at[index]
        )

    old_copy(0).start()
    old_copy(1).start()
    inv_copy = pltpu.make_async_copy(inv_hbm, inv_ref, load_sem.at[0])
    upper_copy = pltpu.make_async_copy(upper_hbm, upper_ref, load_sem.at[1])
    inv_copy.start()
    upper_copy.start()
    for index in range(n_col):
        z_copy(steps - 1, index).start()

    barrier = pltpu.get_barrier_semaphore()

    def greet(to_row, to_col):
        pl.semaphore_signal(
            barrier, inc=1, device_id={"row": to_row, "col": to_col}, device_id_type=MESH
        )

    for hop in range(1, n_col):
        greet(row, lax.rem(col + hop, n_col))
    for other in range(1, ratio):
        greet(base_row * ratio + lax.rem(sub_row + other, ratio), col)
    source_row = col * ratio + sub_row
    for hop in range(n_col):
        source = lax.rem(col + hop, n_col)
        if hop:
            greet(source_row, source)
        else:
            pl.when(jnp.logical_not(has_self))(lambda: greet(source_row, source))

    starts = starts_ref[...]
    offsets = offsets_ref[...]
    mask_rows = math.gcd(old_cols, 512)
    old_first = steps * col_block * n_col + col * old_cols

    def mask_tile(tile, carry):
        rows = pl.ds(pl.multiple_of(tile * mask_rows, mask_rows), mask_rows)
        at = old_first + tile * mask_rows + lax.broadcasted_iota(jnp.int32, (mask_rows, width), 0)
        values = x_old_ref[rows, :].astype(jnp.float32)
        x_live[rows, :] = jnp.where(at < starts, values, 0.0).astype(jnp.bfloat16)
        return carry

    lax.fori_loop(0, old_cols // mask_rows, mask_tile, 0)

    def old_work(index):
        step = steps - 1 - index // OLD_PARTS
        half = index % OLD_PARTS
        slot = index % 2
        depth = math.gcd(old_cut, 512)
        old_copy(index).wait()
        if half == 0:
            old_sum[step] = jnp.zeros((row_block, width), jnp.float32)

        def tile_work(tile, carry):
            at = pl.multiple_of(tile * depth, depth)
            old_sum[step] += jnp.dot(
                old_buf[slot, :, pl.ds(at, depth)],
                x_live[pl.ds(half * old_cut + at, depth), :],
                preferred_element_type=jnp.float32,
            )
            return carry

        lax.fori_loop(0, old_cut // depth, tile_work, 0)
        if index + 2 < steps * OLD_PARTS:
            old_copy(index + 2).start()

    def fold(product):
        return product[:, :width] + product[:, width:]

    def select(step, k):
        places = lax.broadcasted_iota(jnp.int32, (width, width), 0)
        one_hot = jnp.where(places == map_ref[...], 1.0, 0.0).astype(jnp.bfloat16)
        for half in range(2):
            lanes = pl.ds(half * width, width)
            sel[step, :, lanes] = jnp.dot(
                pair_in[k, :, lanes], one_hot, preferred_element_type=jnp.float32
            ).astype(jnp.bfloat16)

    def z_work(step, index):
        tall = 512 if chunk % 512 == 0 else chunk
        z_copy(step, index).wait()

        def tile_work(tile, carry):
            rows = pl.ds(pl.multiple_of(tile * tall, tall), tall)
            value = fold(
                jnp.dot(z_buf[index, rows, :], sel[step], preferred_element_type=jnp.float32)
            )
            if step == steps - 1:
                z_sum[index, rows, :] = value
            else:
                z_sum[index, rows, :] += value
            return carry

        lax.fori_loop(0, chunk // tall, tile_work, 0)
        if step:
            z_copy(step - 1, index).start()

    work = {}
    rounds_each = NEUMANN + 1
    left = list(range(OLD_PARTS, steps * OLD_PARTS))
    for number, index in enumerate(left):
        slot = number * rounds_each // len(left)
        work.setdefault(slot, []).append(functools.partial(old_work, index))
    for step in range(steps - 1, 0, -1):
        for index in range(n_col):
            slot = (steps - step) * rounds_each + index * rounds_each // n_col
            work.setdefault(slot, []).append(functools.partial(z_work, step, index))

    def reduce_rows(k, block):
        copies = []
        for hop in range(n_col - 1, 0, -1):
            target = lax.rem(col + hop, n_col)
            part_out[k, hop - 1] = block(target)
            copy = pltpu.make_async_remote_copy(
                src_ref=part_out.at[k, hop - 1],
                dst_ref=part_in.at[k, hop - 1],
                send_sem=part_send.at[k, hop - 1],
                recv_sem=part_recv.at[k, hop - 1],
                device_id={"row": row, "col": target},
                device_id_type=MESH,
            )
            copy.start()
            copies.append((hop, copy))
        value = block(col)
        for hop, copy in copies:
            copy.wait()
            value = value + part_in[k, hop - 1]
        return value

    passed = []

    def spread(k, value):
        upper = value.astype(jnp.bfloat16)
        lower = (value - upper.astype(jnp.float32)).astype(jnp.bfloat16)
        pair_out[k, :, :width] = upper
        pair_out[k, :, width:] = lower
        for hop in range(groups):
            target = lax.rem(base_row + hop + 1, groups) * ratio + sub_row

            def send():
                pltpu.make_async_remote_copy(
                    src_ref=pair_out.at[k],
                    dst_ref=pair_in.at[k, pl.ds(place, share)],
                    send_sem=pair_send.at[k],
                    recv_sem=pair_recv.at[k, col],
                    device_id={"row": target, "col": owner_col},
                    device_id_type=MESH,
                ).start()

            if hop < groups - 1:
                send()
            else:
                pl.when(jnp.logical_not(has_self))(send)

        @pl.when(has_self)
        def _():
            pair_in[k, pl.ds(place, share), :width] = upper
            pair_in[k, pl.ds(place, share), width:] = lower

        for task in work.get(k, ()):
            task()
        arriving = []
        for hop in range(n_col):
            source = lax.rem(col + hop, n_col)
            at = pl.multiple_of(sub_row * row_block + source * share, share)
            span = pair_in.at[k, pl.ds(at, share)]

            def arrived():
                pltpu.make_async_copy(span, span, pair_recv.at[k, source]).wait()

            if hop:
                arrived()
            else:
                pl.when(jnp.logical_not(has_self))(arrived)
            for other in range(1, ratio):
                copy = pltpu.make_async_remote_copy(
                    src_ref=span,
                    dst_ref=span,
                    send_sem=pass_send.at[k, other - 1, hop],
                    recv_sem=pass_recv.at[k, other - 1, hop],
                    device_id={"row": base_row * ratio + lax.rem(sub_row + other, ratio), "col": col},
                    device_id_type=MESH,
                )
                copy.start()
                arriving.append(copy)
        for copy in arriving:
            copy.wait_recv()
        passed.extend(arriving)

    def times(mat_ref, index, k):
        def block(target):
            rows = pl.ds(pl.multiple_of(target * share, share), share)
            return fold(
                jnp.dot(mat_ref[index, rows, :], pair_in[k], preferred_element_type=jnp.float32)
            )

        return block

    for index in range(OLD_PARTS):
        old_work(index)
    pl.semaphore_wait(barrier, n_col - 1 + ratio - 1 + groups - jnp.where(has_self, 1, 0))

    k = 0
    solved_at = {}
    for step in reversed(range(steps)):

        def rhs_block(target):
            rows = pl.ds(pl.multiple_of(target * share, share), share)
            value = -old_sum[step, rows, :]
            for later in range(step + 1, steps):
                value = value - times(upper_ref, pairs[step, later], solved_at[later])(target)
            return value

        mine = pl.ds(pl.multiple_of(col * share, share), share)
        rhs = reduce_rows(k, rhs_block) + forcing_ref[step, mine, :]
        spread(k, rhs)
        k += 1
        if step == steps - 1:
            inv_copy.wait()
            upper_copy.wait()
        total = None
        for term_index in range(NEUMANN):
            term = reduce_rows(k, times(inv_ref, step, k - 1))
            if term_index:
                term = term * offsets
            total = term if total is None else total + term
            if term_index < NEUMANN - 1:
                spread(k, term)
                k += 1
        first = step * (col_block * n_col) + row * row_block + col * share
        rows = first + lax.broadcasted_iota(jnp.int32, (share, width), 0)
        total = jnp.where(rows < starts, total, 0.0)
        solved_ref[step] = total
        spread(k, total)
        solved_at[step] = k
        select(step, k)
        k += 1

    n_pairs = n_col // 2
    half_col = lax.rem(col, 2)
    pair_col = col // 2
    piece = chunk // PIECES
    to_wait = []
    for turn in range(n_pairs):
        target_pair = lax.rem(pair_col + 1 + turn, n_pairs)
        theirs = target_pair * 2 + 1 - half_col
        ours = target_pair * 2 + half_col
        z_work(0, theirs)
        copies = []
        for part in range(PIECES):
            span = pl.ds(part * piece, piece)
            copy = pltpu.make_async_remote_copy(
                src_ref=z_sum.at[theirs, span],
                dst_ref=core_in.at[turn, span],
                send_sem=core_send.at[turn, part],
                recv_sem=core_recv.at[turn, part],
                device_id={"row": row, "col": pair_col * 2 + 1 - half_col},
                device_id_type=MESH,
            )
            copy.start()
            copies.append(copy)
        to_wait.extend(copies)
        z_work(0, ours)
        for part in range(PIECES):
            span = pl.ds(part * piece, piece)
            copies[part].wait_recv()
            if turn == n_pairs - 1:
                acc_out_ref[span, :] = (
                    acc_ref[span, :] + z_sum[ours, span, :] + core_in[turn, span, :]
                )
            else:
                core_in[turn, span, :] += z_sum[ours, span, :]
                copy = pltpu.make_async_remote_copy(
                    src_ref=core_in.at[turn, span],
                    dst_ref=chip_in.at[turn, span],
                    send_sem=chip_send.at[turn, part],
                    recv_sem=chip_recv.at[turn, part],
                    device_id={"row": row, "col": ours},
                    device_id_type=MESH,
                )
                copy.start()
                to_wait.append((copy, turn, span))
    for entry in to_wait:
        if isinstance(entry, tuple):
            copy, turn, span = entry
            copy.wait_recv()
            acc_out_ref[span, :] += chip_in[turn, span, :]
            copy.wait_send()
        else:
            entry.wait_send()
    for copy in passed:
        copy.wait_send()
    for slot in range(k):
        for mine, count in ((True, groups - 1), (False, groups)):

            @pl.when(has_self == mine)
            def _():
                span = pair_in.at[slot, pl.ds(0, count * share)]
                pltpu.make_async_copy(span, span, pair_send.at[slot]).wait()


def chain(n_row, n_col, t_upper, inverses, t_old, by_step, forcing, x_old, offsets, starts, column_map, acc):
    steps, row_block, width = forcing.shape
    col_block = t_upper.shape[2]
    share = row_block // n_col
    ratio = col_block // row_block
    rounds = steps * (NEUMANN + 1)
    old_cols = x_old.shape[0]
    chunk = by_step.shape[1] // n_col
    n_pairs = n_col // 2
    far = max(n_pairs - 1, 1)
    near = max(ratio - 1, 1)
    vmem = pl.BlockSpec(memory_space=pltpu.VMEM)
    hbm = pl.BlockSpec(memory_space=pl.ANY)
    dma = pltpu.SemaphoreType.DMA
    return pl.pallas_call(
        functools.partial(chain_kernel, n_row, n_col),
        out_shape=(
            jax.ShapeDtypeStruct((steps, share, width), jnp.float32),
            jax.ShapeDtypeStruct(acc.shape, jnp.float32),
        ),
        in_specs=[hbm] * 4 + [vmem] * 6,
        out_specs=(vmem, vmem),
        scratch_shapes=[
            pltpu.VMEM(t_upper.shape, jnp.bfloat16),
            pltpu.VMEM(inverses.shape, jnp.bfloat16),
            pltpu.VMEM((2, row_block, old_cols // OLD_PARTS), jnp.bfloat16),
            pltpu.VMEM((n_col, chunk, col_block), jnp.bfloat16),
            pltpu.VMEM((old_cols, width), jnp.bfloat16),
            pltpu.VMEM((steps, row_block, width), jnp.float32),
            pltpu.VMEM((steps, col_block, 2 * width), jnp.bfloat16),
            pltpu.VMEM((n_col, chunk, width), jnp.float32),
            pltpu.VMEM((rounds, n_col - 1, share, width), jnp.float32),
            pltpu.VMEM((rounds, n_col - 1, share, width), jnp.float32),
            pltpu.VMEM((rounds, share, 2 * width), jnp.bfloat16),
            pltpu.VMEM((rounds, col_block, 2 * width), jnp.bfloat16),
            pltpu.VMEM((n_pairs, chunk, width), jnp.float32),
            pltpu.VMEM((far, chunk, width), jnp.float32),
            dma((2,)),
            dma((2,)),
            dma((n_col,)),
            dma((rounds, n_col - 1)),
            dma((rounds, n_col - 1)),
            dma((rounds,)),
            dma((rounds, n_col)),
            dma((rounds, near, n_col)),
            dma((rounds, near, n_col)),
            dma((n_pairs, PIECES)),
            dma((n_pairs, PIECES)),
            dma((far, PIECES)),
            dma((far, PIECES)),
        ],
        compiler_params=pltpu.CompilerParams(
            collective_id=0, has_side_effects=True, vmem_limit_bytes=58 * 1024 * 1024
        ),
        name="chain",
    )(
        t_upper, inverses, t_old, by_step, forcing, x_old,
        offsets[None, :], starts[None, :], column_map[None, :], acc,
    )


def body(t_upper, t_old, inverses, forcing, x_old, offsets, starts, column_map, z_cols, acc):
    n_col = lax.axis_size("col")
    n_row = lax.axis_size("row")
    by_step = jnp.transpose(z_cols, (1, 0, 2))
    return chain(
        n_row, n_col, t_upper, inverses, t_old, by_step, forcing, x_old,
        offsets, starts, column_map, acc,
    )


def solution(mesh):
    placed = (
        P(None, "row", "col"),
        P(None, "row", "col"),
        P(None, "row", "col"),
        P(None, "row", None),
        P("col", None),
        P(),
        P(),
        P(),
        P("row", None, "col"),
        P(("row", "col"), None),
    )
    return jax.shard_map(
        body,
        mesh=mesh,
        in_specs=placed,
        out_specs=(P(None, ("row", "col"), None), P(("row", "col"), None)),
        check_vma=False,
    )
```

```python
import functools
import math

import jax
import jax.numpy as jnp
from jax import lax
from jax.experimental import pallas as pl
from jax.experimental.pallas import tpu as pltpu
from jax.sharding import PartitionSpec as P

NEUMANN = 3
PIECES = 4
OLD_PARTS = 2
MESH = pl.DeviceIdType.MESH


def pair_indices(steps):
    pairs = {}
    for first in range(steps):
        for second in range(first + 1, steps):
            pairs[first, second] = len(pairs)
    return pairs


def chain_kernel(
    n_row, n_col,
    upper_hbm, inv_hbm, old_hbm, z_hbm,
    forcing_ref, x_old_ref, offsets_ref, starts_ref, starts_flat, map_ref, acc_ref,
    solved_ref, acc_out_ref,
    upper_ref, inv_ref, old_buf, z_buf, x_live, old_sum, sel, z_sum,
    part_out, part_in, pair_out, pair_in, core_in, chip_in,
    load_sem, old_sem, z_sem,
    part_send, part_recv, pair_send, pair_recv, pass_send, pass_recv,
    core_send, core_recv, chip_send, chip_recv,
):
    row = lax.axis_index("row")
    col = lax.axis_index("col")
    steps, row_block, width = forcing_ref.shape
    col_block = upper_ref.shape[2]
    share = row_block // n_col
    ratio = col_block // row_block
    old_cols = x_old_ref.shape[0]
    chunk = z_sum.shape[1]
    pairs = pair_indices(steps)
    base_row = row // ratio
    sub_row = lax.rem(row, ratio)
    owner_col = base_row
    has_self = owner_col == col
    groups = n_row // ratio
    place = pl.multiple_of(sub_row * row_block + col * share, share)

    old_cut = old_cols // OLD_PARTS

    def old_copy(index):
        step = steps - 1 - index // OLD_PARTS
        half = index % OLD_PARTS
        slot = index % 2
        return pltpu.make_async_copy(
            old_hbm.at[step, :, pl.ds(half * old_cut, old_cut)], old_buf.at[slot], old_sem.at[slot]
        )

    def z_copy(step, index):
        first = index * chunk
        if not isinstance(index, int):
            first = pl.multiple_of(first, chunk)
        return pltpu.make_async_copy(
            z_hbm.at[step, pl.ds(first, chunk)], z_buf.at[index], z_sem.at[index]
        )

    old_copy(0).start()
    old_copy(1).start()
    inv_copy = pltpu.make_async_copy(inv_hbm, inv_ref, load_sem.at[0])
    upper_copy = pltpu.make_async_copy(upper_hbm, upper_ref, load_sem.at[1])
    inv_copy.start()
    upper_copy.start()
    for index in range(n_col):
        z_copy(steps - 1, index).start()

    barrier = pltpu.get_barrier_semaphore()

    def greet(to_row, to_col):
        pl.semaphore_signal(
            barrier, inc=1, device_id={"row": to_row, "col": to_col}, device_id_type=MESH
        )

    for hop in range(1, n_col):
        greet(row, lax.rem(col + hop, n_col))
    for other in range(1, ratio):
        greet(base_row * ratio + lax.rem(sub_row + other, ratio), col)
    source_row = col * ratio + sub_row
    for hop in range(n_col):
        source = lax.rem(col + hop, n_col)
        if hop:
            greet(source_row, source)
        else:
            pl.when(jnp.logical_not(has_self))(lambda: greet(source_row, source))

    starts = starts_flat[...]
    mask_rows = math.gcd(old_cols, 512)
    old_first = steps * col_block * n_col + col * old_cols

    def mask_tile(tile, carry):
        rows = pl.ds(pl.multiple_of(tile * mask_rows, mask_rows), mask_rows)
        at = old_first + tile * mask_rows + lax.broadcasted_iota(jnp.int32, (mask_rows, width), 0)
        values = x_old_ref[rows, :].astype(jnp.float32)
        x_live[rows, :] = jnp.where(at < starts, values, 0.0).astype(jnp.bfloat16)
        return carry

    lax.fori_loop(0, old_cols // mask_rows, mask_tile, 0)

    def old_work(index):
        step = steps - 1 - index // OLD_PARTS
        half = index % OLD_PARTS
        slot = index % 2
        depth = math.gcd(old_cut, 512)
        old_copy(index).wait()
        if half == 0:
            old_sum[step] = jnp.zeros((row_block, width), jnp.float32)

        def tile_work(tile, carry):
            at = pl.multiple_of(tile * depth, depth)
            old_sum[step] += jnp.dot(
                old_buf[slot, :, pl.ds(at, depth)],
                x_live[pl.ds(half * old_cut + at, depth), :],
                preferred_element_type=jnp.float32,
            )
            return carry

        lax.fori_loop(0, old_cut // depth, tile_work, 0)
        if index + 2 < steps * OLD_PARTS:
            old_copy(index + 2).start()

    def fold(product):
        return product[:, :width] + product[:, width:]

    half = width // 2
    packed_rows = share // 2
    lanes = lax.broadcasted_iota(jnp.int32, (packed_rows, width), 1)
    in_front = lanes < half

    def turned(value):
        return pltpu.roll(value, half, 1)

    def pack(value, side):
        front, back = value[:packed_rows], value[packed_rows:]
        if side:
            return jnp.where(in_front, turned(front), back)
        return jnp.where(in_front, front, turned(back))

    def pack_product(product):
        both = product + turned(product)
        return jnp.where(in_front, both[:packed_rows], both[packed_rows:])

    def select(step, k):
        lane = lax.broadcasted_iota(jnp.int32, (width, 2 * width), 0)
        is_low = lax.broadcasted_iota(jnp.int32, (width, 2 * width), 1) >= width
        wanted = jnp.concatenate([map_ref[...], map_ref[...]], axis=1)
        picked = None
        for side in range(2):
            column = wanted - side * half
            inside = jnp.logical_and(column >= 0, column < half)
            place = jnp.where(is_low, column + half, column)
            hit = jnp.logical_and(inside, lane == place)
            one_hot = jnp.where(hit, 1.0, 0.0).astype(jnp.bfloat16)
            value = jnp.dot(pair_in[2 * k + side], one_hot, preferred_element_type=jnp.float32)
            picked = value if picked is None else picked + value
        sel[step] = picked.astype(jnp.bfloat16)

    def z_work(step, index):
        tall = 512 if chunk % 512 == 0 else chunk
        z_copy(step, index).wait()

        def tile_work(tile, carry):
            rows = pl.ds(pl.multiple_of(tile * tall, tall), tall)
            value = fold(
                jnp.dot(z_buf[index, rows, :], sel[step], preferred_element_type=jnp.float32)
            )
            if step == steps - 1:
                z_sum[index, rows, :] = value
            else:
                z_sum[index, rows, :] += value
            return carry

        lax.fori_loop(0, chunk // tall, tile_work, 0)
        if step:
            z_copy(step - 1, index).start()

    work = {}
    rounds_each = NEUMANN + 1
    left = list(range(OLD_PARTS, steps * OLD_PARTS))
    for number, index in enumerate(left):
        slot = number * rounds_each // len(left)
        work.setdefault(slot, []).append(functools.partial(old_work, index))
    for step in range(steps - 1, 0, -1):
        for index in range(n_col):
            slot = (steps - step) * rounds_each + index * rounds_each // n_col
            if index == 0:
                solved_slot = (steps - step) * rounds_each - 1
                work.setdefault(slot, []).append(functools.partial(select, step, solved_slot))
            work.setdefault(slot, []).append(functools.partial(z_work, step, index))

    def reduce_start(s, block):
        copies = []
        for hop in range(n_col - 1, 0, -1):
            target = lax.rem(col + hop, n_col)
            part_out[s, hop - 1] = block(target)
            copy = pltpu.make_async_remote_copy(
                src_ref=part_out.at[s, hop - 1],
                dst_ref=part_in.at[s, hop - 1],
                send_sem=part_send.at[s, hop - 1],
                recv_sem=part_recv.at[s, hop - 1],
                device_id={"row": row, "col": target},
                device_id_type=MESH,
            )
            copy.start()
            copies.append((hop, copy))
        return block(col), copies

    def reduce_finish(s, started):
        value, copies = started
        for hop, copy in reversed(copies):
            copy.wait_recv()
            value = value + part_in[s, hop - 1]
        to_end.extend(copy for _, copy in copies)
        return value

    def spread_start(s, value):
        upper = value.astype(jnp.bfloat16).astype(jnp.float32)
        lower = value - upper
        front = jnp.where(in_front, upper, turned(lower)).astype(jnp.bfloat16)
        back = jnp.where(in_front, turned(upper), lower).astype(jnp.bfloat16)
        pair_out[s, :packed_rows] = front
        pair_out[s, packed_rows:] = back
        for hop in range(groups):
            target = lax.rem(base_row + hop + 1, groups) * ratio + sub_row

            def send():
                pltpu.make_async_remote_copy(
                    src_ref=pair_out.at[s],
                    dst_ref=pair_in.at[s, pl.ds(place, share)],
                    send_sem=pair_send.at[s],
                    recv_sem=pair_recv.at[s, col],
                    device_id={"row": target, "col": owner_col},
                    device_id_type=MESH,
                ).start()

            if hop < groups - 1:
                send()
            else:
                pl.when(jnp.logical_not(has_self))(send)

        @pl.when(has_self)
        def _():
            pair_in[s, pl.ds(place, share)] = jnp.concatenate([front, back], axis=0)

    def pass_on(s):
        for hop in range(n_col):
            source = lax.rem(col + hop, n_col)
            at = pl.multiple_of(sub_row * row_block + source * share, share)
            span = pair_in.at[s, pl.ds(at, share)]

            def arrived():
                pltpu.make_async_copy(span, span, pair_recv.at[s, source]).wait()

            if hop:
                arrived()
            else:
                pl.when(jnp.logical_not(has_self))(arrived)
            for other in range(1, ratio):
                pltpu.make_async_remote_copy(
                    src_ref=span,
                    dst_ref=span,
                    send_sem=pass_send.at[s, other - 1],
                    recv_sem=pass_recv.at[s, other - 1],
                    device_id={"row": base_row * ratio + lax.rem(sub_row + other, ratio), "col": col},
                    device_id_type=MESH,
                ).start()

    def pass_wait(s, sem, towards):
        for other in range(1, ratio):
            source = lax.rem(sub_row + (ratio - other if towards else 0), ratio)
            at = pl.multiple_of(source * row_block, row_block)
            span = pair_in.at[s, pl.ds(at, row_block)]
            pltpu.make_async_copy(span, span, sem.at[s, other - 1]).wait()

    def times(mat_ref, index, s):
        def block(target):
            rows = pl.ds(pl.multiple_of(target * share, share), share)
            return pack_product(
                jnp.dot(mat_ref[index, rows, :], pair_in[s], preferred_element_type=jnp.float32)
            )

        return block

    to_end = []
    totals = {}

    def run(side):
        offsets = offsets_ref[side]
        starts = starts_ref[side]
        solved_at = {}
        s = side
        for step in reversed(range(steps)):

            def rhs_block(target):
                rows = pl.ds(pl.multiple_of(target * share, share), share)
                value = -pack(old_sum[step, rows, :], side)
                for later in range(step + 1, steps):
                    value = value - times(upper_ref, pairs[step, later], solved_at[later])(target)
                return value

            total = None
            for phase in range(NEUMANN + 1):
                if phase == 0:
                    started = reduce_start(s, rhs_block)
                else:
                    started = reduce_start(s, times(inv_ref, step, s - 2))
                yield
                value = reduce_finish(s, started)
                if phase == 0:
                    mine = pl.ds(pl.multiple_of(col * share, share), share)
                    value = value + pack(forcing_ref[step, mine, :], side)
                elif phase > 1:
                    value = value * offsets
                if phase:
                    total = value if total is None else total + value
                if phase < NEUMANN:
                    spread_start(s, value)
                    yield
                    pass_on(s)
                    yield
                    pass_wait(s, pass_recv, True)
                    s += 2
            first = step * (col_block * n_col) + row * row_block + col * share
            rows = first + lax.broadcasted_iota(jnp.int32, (packed_rows, width), 0)
            rows = rows + jnp.where(in_front, 0, packed_rows)
            total = jnp.where(rows < starts, total, 0.0)
            totals[step, side] = total
            spread_start(s, total)
            solved_at[step] = s
            yield
            pass_on(s)
            yield
            pass_wait(s, pass_recv, True)
            s += 2

    for index in range(OLD_PARTS):
        old_work(index)
    inv_copy.wait()
    upper_copy.wait()
    pl.semaphore_wait(barrier, n_col - 1 + ratio - 1 + groups - jnp.where(has_self, 1, 0))

    sides = [run(0), run(1)]
    for k in range(steps * rounds_each):
        for stage in range(3):
            for side in sides:
                next(side)
            if stage == 1:
                for task in work.get(k, ()):
                    task()
                if k % rounds_each == NEUMANN:
                    step = steps - 1 - k // rounds_each
                    one, two = totals[step, 0], totals[step, 1]
                    solved_ref[step, :packed_rows] = jnp.where(in_front, one, turned(two))
                    solved_ref[step, packed_rows:] = jnp.where(in_front, turned(one), two)
    for side in sides:
        assert next(side, None) is None
    select(0, steps * rounds_each - 1)

    n_pairs = n_col // 2
    half_col = lax.rem(col, 2)
    pair_col = col // 2
    piece = chunk // PIECES
    to_wait = []
    for turn in range(n_pairs):
        target_pair = lax.rem(pair_col + 1 + turn, n_pairs)
        theirs = target_pair * 2 + 1 - half_col
        ours = target_pair * 2 + half_col
        z_work(0, theirs)
        copies = []
        for part in range(PIECES):
            span = pl.ds(part * piece, piece)
            copy = pltpu.make_async_remote_copy(
                src_ref=z_sum.at[theirs, span],
                dst_ref=core_in.at[turn, span],
                send_sem=core_send.at[turn, part],
                recv_sem=core_recv.at[turn, part],
                device_id={"row": row, "col": pair_col * 2 + 1 - half_col},
                device_id_type=MESH,
            )
            copy.start()
            copies.append(copy)
        to_wait.extend(copies)
        z_work(0, ours)
        for part in range(PIECES):
            span = pl.ds(part * piece, piece)
            copies[part].wait_recv()
            if turn == n_pairs - 1:
                acc_out_ref[span, :] = (
                    acc_ref[span, :] + z_sum[ours, span, :] + core_in[turn, span, :]
                )
            else:
                core_in[turn, span, :] += z_sum[ours, span, :]
                copy = pltpu.make_async_remote_copy(
                    src_ref=core_in.at[turn, span],
                    dst_ref=chip_in.at[turn, span],
                    send_sem=chip_send.at[turn, part],
                    recv_sem=chip_recv.at[turn, part],
                    device_id={"row": row, "col": ours},
                    device_id_type=MESH,
                )
                copy.start()
                to_wait.append((copy, turn, span))
    for entry in to_wait:
        if isinstance(entry, tuple):
            copy, turn, span = entry
            copy.wait_recv()
            acc_out_ref[span, :] += chip_in[turn, span, :]
            copy.wait_send()
        else:
            entry.wait_send()
    for copy in to_end:
        copy.wait_send()
    for slot in range(2 * steps * rounds_each):
        pass_wait(slot, pass_send, False)
        for mine, count in ((True, groups - 1), (False, groups)):

            @pl.when(has_self == mine)
            def _():
                span = pair_in.at[slot, pl.ds(0, count * share)]
                pltpu.make_async_copy(span, span, pair_send.at[slot]).wait()


def chain(n_row, n_col, t_upper, inverses, t_old, by_step, forcing, x_old, offsets, starts, column_map, acc):
    steps, row_block, width = forcing.shape
    col_block = t_upper.shape[2]
    share = row_block // n_col
    ratio = col_block // row_block
    slots = 2 * steps * (NEUMANN + 1)
    old_cols = x_old.shape[0]
    chunk = by_step.shape[1] // n_col
    n_pairs = n_col // 2
    far = max(n_pairs - 1, 1)
    near = max(ratio - 1, 1)

    def by_side(values):
        halves = values.reshape(2, 1, width // 2)
        return jnp.concatenate([halves, halves], axis=2)

    vmem = pl.BlockSpec(memory_space=pltpu.VMEM)
    hbm = pl.BlockSpec(memory_space=pl.ANY)
    dma = pltpu.SemaphoreType.DMA
    return pl.pallas_call(
        functools.partial(chain_kernel, n_row, n_col),
        out_shape=(
            jax.ShapeDtypeStruct((steps, share, width), jnp.float32),
            jax.ShapeDtypeStruct(acc.shape, jnp.float32),
        ),
        in_specs=[hbm] * 4 + [vmem] * 7,
        out_specs=(vmem, vmem),
        scratch_shapes=[
            pltpu.VMEM(t_upper.shape, jnp.bfloat16),
            pltpu.VMEM(inverses.shape, jnp.bfloat16),
            pltpu.VMEM((2, row_block, old_cols // OLD_PARTS), jnp.bfloat16),
            pltpu.VMEM((n_col, chunk, col_block), jnp.bfloat16),
            pltpu.VMEM((old_cols, width), jnp.bfloat16),
            pltpu.VMEM((steps, row_block, width), jnp.float32),
            pltpu.VMEM((steps, col_block, 2 * width), jnp.bfloat16),
            pltpu.VMEM((n_col, chunk, width), jnp.float32),
            pltpu.VMEM((slots, n_col - 1, share // 2, width), jnp.float32),
            pltpu.VMEM((slots, n_col - 1, share // 2, width), jnp.float32),
            pltpu.VMEM((slots, share, width), jnp.bfloat16),
            pltpu.VMEM((slots, col_block, width), jnp.bfloat16),
            pltpu.VMEM((n_pairs, chunk, width), jnp.float32),
            pltpu.VMEM((far, chunk, width), jnp.float32),
            dma((2,)),
            dma((2,)),
            dma((n_col,)),
            dma((slots, n_col - 1)),
            dma((slots, n_col - 1)),
            dma((slots,)),
            dma((slots, n_col)),
            dma((slots, near)),
            dma((slots, near)),
            dma((n_pairs, PIECES)),
            dma((n_pairs, PIECES)),
            dma((far, PIECES)),
            dma((far, PIECES)),
        ],
        compiler_params=pltpu.CompilerParams(
            collective_id=0, has_side_effects=True, vmem_limit_bytes=58 * 1024 * 1024
        ),
        name="chain",
    )(
        t_upper, inverses, t_old, by_step, forcing, x_old,
        by_side(offsets), by_side(starts), starts[None, :], column_map[None, :], acc,
    )


def body(t_upper, t_old, inverses, forcing, x_old, offsets, starts, column_map, z_cols, acc):
    n_col = lax.axis_size("col")
    n_row = lax.axis_size("row")
    by_step = jnp.transpose(z_cols, (1, 0, 2))
    return chain(
        n_row, n_col, t_upper, inverses, t_old, by_step, forcing, x_old,
        offsets, starts, column_map, acc,
    )


def solution(mesh):
    placed = (
        P(None, "row", "col"),
        P(None, "row", "col"),
        P(None, "row", "col"),
        P(None, "row", None),
        P("col", None),
        P(),
        P(),
        P(),
        P("row", None, "col"),
        P(("row", "col"), None),
    )
    return jax.shard_map(
        body,
        mesh=mesh,
        in_specs=placed,
        out_specs=(P(None, ("row", "col"), None), P(("row", "col"), None)),
        check_vma=False,
    )
```
